256 devices in a mesh: tile: 64 (over z, x, core), grp: 4 (over y).
Axes of the slice: x: 4, y: 4, z: 8, core: 2. Of those that a mesh axis runs over, the one named last changes fastest.
Arguments:
- observations: bfloat16 [1048576, 256], P(('tile', 'grp')), may hold values from -6 to 6
- obs_key_weight: bfloat16 [256, 512], replicated, may hold values from -0.375 to 0.375
- obs_value_weight: bfloat16 [256, 512], replicated, may hold values from -0.375 to 0.375
- background: bfloat16 [65536, 512], P(('tile', 'grp')), may hold values from -6 to 6
- query_weight: bfloat16 [512, 512], replicated, may hold values from -2.1213203 to 2.1213203
- key_weight: bfloat16 [512, 512], replicated, may hold values from -0.25 to 0.25
- value_weight: bfloat16 [512, 512], replicated, may hold values from -0.25 to 0.25
- out_weight: bfloat16 [512, 512], replicated, may hold values from -0.25 to 0.25
- owners: int32 [256, 32], replicated, may hold values from 0 to 63, as said below
- attend_list: int32 [512, 32], P(('tile', 'grp')), may hold values from -1 to 63, as said below
- obs_count: int32 [256], replicated, may hold values from 2048 to 4096, as said below
Outputs:
- updated: bfloat16 [65536, 512], P(('tile', 'grp'))
The draws below stay inside these ranges and needn't reach their ends.
Inputs may be any that keep to these rules, and one draw needn't show every extreme that they name: `owners`: each ingest device sends to each tile either none or exactly 1 of its blocks, in any order among its blocks; its own tile (d // 4) always gets 1. `attend_list`: every block that a device's tile owns among ingest devices of the device's grp index is named exactly once among the device's 2 rows; valid entries come first in each row, -1 marks an empty entry. `obs_count`: the valid rows of an ingest device are its leading rows.
All inputs are finite; a program needn't handle non-finite values.
Results may differ from the reference program's by a relative error of at most 0.0078.
Values may be sent and summed in bfloat16 or wider, within the bound.
A program may use at most 128 MiB of HBM per device.

```python
import math
import jax
import jax.numpy as jnp
from jax import lax

CH = 256
HEADS = 8
HDIM = 64
WIDTH = 512
BLOCK = 128
OBS_BLK = 32
Q_DEV = 256
CAP = 1
PICK = 32
HOT = 10
QB = 2
ATT = 32
OBS_ROWS = 1048576
LAT_ROWS = 65536
N_TILE = 64
N_GRP = 4


def owner_table(key):
    device_count = N_TILE * N_GRP
    hot_order = jax.random.permutation(jax.random.fold_in(key, 1), N_TILE).astype(jnp.int32)
    hot_flag = (hot_order < HOT).astype(jnp.int32)
    row_keys = jax.random.split(jax.random.fold_in(key, 2), device_count)
    jitter = jax.vmap(lambda subkey: jax.random.permutation(subkey, N_TILE))(row_keys).astype(jnp.int32)
    own_flag = ((jnp.arange(device_count, dtype=jnp.int32) // N_GRP)[:, None] == jnp.arange(N_TILE, dtype=jnp.int32)[None, :]).astype(jnp.int32)
    score = jitter + 2 * N_TILE * hot_flag[None, :] + N_TILE * own_flag
    picked = lax.top_k(score, PICK)[1].astype(jnp.int32)
    order_keys = jax.random.split(jax.random.fold_in(key, 3), device_count)
    order = jax.vmap(lambda subkey: jax.random.permutation(subkey, OBS_BLK))(order_keys).astype(jnp.int32)
    return jnp.take_along_axis(picked, order // CAP, axis=1).astype(jnp.int32)


def draw_owners(key, part):
    return owner_table(jax.random.fold_in(key, 17))


def draw_attend_list(key, part):
    owner_rows = owner_table(jax.random.fold_in(key, 17))
    device_count = N_TILE * N_GRP
    slot_count = N_TILE * CAP
    shuffle = jax.random.permutation(jax.random.fold_in(key, 23), slot_count).astype(jnp.int32)
    tile_range = jnp.arange(N_TILE, dtype=jnp.int32)

    def one_device(device):
        tile_index = device // N_GRP
        group_index = device % N_GRP
        sources = tile_range * N_GRP + group_index
        column = jnp.take(owner_rows, sources, axis=0)
        sent = jnp.sum((column == tile_index).astype(jnp.int32), axis=1)
        owned = (jnp.arange(CAP, dtype=jnp.int32)[None, :] < sent[:, None]).reshape(slot_count)
        score = shuffle + slot_count * owned.astype(jnp.int32)
        ordered = lax.top_k(score, slot_count)[1].astype(jnp.int32)
        chosen = jnp.where(jnp.take(owned, ordered), ordered, -1)
        return chosen.reshape(ATT, QB).T
    lists = jax.vmap(one_device)(jnp.arange(device_count, dtype=jnp.int32))
    return lists.reshape(device_count * QB, ATT).astype(jnp.int32)


def draw_obs_count(key, part):
    device_count = N_TILE * N_GRP
    full_rows = OBS_BLK * BLOCK
    counts = jax.random.randint(jax.random.fold_in(key, 5), (device_count,), full_rows // 2, full_rows + 1)
    chosen = jax.random.randint(jax.random.fold_in(key, 6), (), 0, device_count)
    positions = jnp.arange(device_count, dtype=jnp.int32)
    counts = jnp.where(positions == chosen, full_rows, counts)
    counts = jnp.where(positions == (chosen + 1) % device_count, full_rows // 2, counts)
    return counts.astype(jnp.int32)


def draw_query_weight(key, part):
    head_rank = jax.random.permutation(jax.random.fold_in(key, 31), HEADS).astype(jnp.float32)
    level = jnp.exp(head_rank * (math.log(8.0) / max(1, HEADS - 1)))
    column_level = jnp.repeat(level, HDIM)
    base = jnp.clip(jax.random.normal(jax.random.fold_in(key, 37), (WIDTH, WIDTH), jnp.float32), -6.0, 6.0)
    scaled = base * column_level[None, :] * float(WIDTH) ** (-0.5)
    return scaled.astype(jnp.bfloat16)


def steps_of(key, extent, cuts, low, high):
    loudness, own = 1.0, jax.random.fold_in(key, 6)
    for position, blocks in cuts:
        steps = jnp.exp(jax.random.uniform(jax.random.fold_in(own, position), (blocks,), jnp.float32, low / len(cuts), high / len(cuts)))
        loudness = loudness * jnp.repeat(steps, extent[position] // blocks).reshape([-1 if axis == position else 1 for axis in range(len(extent))])
    return loudness


def gaussian(stream_key, dims, spread, reach, cuts=(), kind=jnp.bfloat16):
    result = spread * jax.random.normal(stream_key, dims, jnp.float32)
    if cuts:
        result = result * steps_of(stream_key, dims, cuts, -0.22, 0.18)
    return jnp.clip(result, -reach, reach).astype(kind)


def setup_inputs(seed: int = 0) -> dict:
    key_list = jax.random.split(jax.random.key(seed), 12)
    return {
        "observations": gaussian(key_list[0], (OBS_ROWS, CH), 1.0, 6.0, ((0, 256),)),
        "obs_key_weight": gaussian(key_list[1], (CH, WIDTH), CH ** -0.5, 0.375),
        "obs_value_weight": gaussian(key_list[2], (CH, WIDTH), CH ** -0.5, 0.375),
        "background": gaussian(key_list[3], (LAT_ROWS, WIDTH), 1.0, 6.0, ((0, 256),)),
        "query_weight": draw_query_weight(jax.random.fold_in(key_list[11], 71), 0),
        "key_weight": gaussian(key_list[5], (WIDTH, WIDTH), WIDTH ** -0.5, 0.25),
        "value_weight": gaussian(key_list[6], (WIDTH, WIDTH), WIDTH ** -0.5, 0.25),
        "out_weight": gaussian(key_list[7], (WIDTH, WIDTH), WIDTH ** -0.5, 0.25),
        "owners": draw_owners(jax.random.fold_in(key_list[11], 71), 0),
        "attend_list": draw_attend_list(jax.random.fold_in(key_list[11], 71), 0),
        "obs_count": draw_obs_count(jax.random.fold_in(key_list[11], 71), 0),
    }


SOFT_LIMIT = 20.0
EPSILON = 1e-06

def project(rows, weight):
    return jnp.dot(rows, weight, preferred_element_type=jnp.float32).astype(jnp.bfloat16)

def block_ranks(owner_rows):
    count = owner_rows.shape[-1]
    positions = jnp.arange(count, dtype=jnp.int32)
    same_owner = owner_rows[..., :, None] == owner_rows[..., None, :]
    earlier = positions[None, :] < positions[:, None]
    return lax.optimization_barrier(jnp.sum((same_owner & earlier).astype(jnp.int32), axis=-1))

def located_block(owner_rows, tile_index, rank_of):
    positions = jnp.arange(owner_rows.shape[-1], dtype=jnp.int32)
    matches = (owner_rows == tile_index) & (block_ranks(owner_rows) == rank_of[..., None])
    return lax.optimization_barrier(jnp.sum(jnp.where(matches, positions, 0), axis=-1)).astype(jnp.int32)

def reference(observations, obs_key_weight, obs_value_weight, background, query_weight, key_weight, value_weight, out_weight, owners, attend_list, obs_count):
    blocks = observations.reshape(N_TILE * N_GRP * OBS_BLK, BLOCK, CH)
    latent_rows = N_GRP * Q_DEV

    def one_device(device):
        device = device.astype(jnp.int32)
        tile_index = device // N_GRP
        group_index = device % N_GRP
        own_rows = lax.dynamic_slice_in_dim(background, device * Q_DEV, Q_DEV, 0)
        tile_rows = lax.dynamic_slice_in_dim(background, tile_index * latent_rows, latent_rows, 0)
        queries = project(own_rows, query_weight).reshape(QB, BLOCK, HEADS, HDIM)
        tile_keys = project(tile_rows, key_weight).reshape(latent_rows, HEADS, HDIM)
        tile_values = project(tile_rows, value_weight).reshape(latent_rows, HEADS, HDIM)
        list_rows = lax.dynamic_slice_in_dim(attend_list, device * QB, QB, 0)
        present = list_rows >= 0
        slot_ids = jnp.maximum(list_rows, 0)
        source_device = (slot_ids // CAP * N_GRP + group_index).astype(jnp.int32)
        source_owners = jnp.take(owners, source_device, axis=0)
        block_index = located_block(source_owners, tile_index, slot_ids % CAP)
        chosen = jnp.take(blocks, source_device * OBS_BLK + block_index, axis=0)
        flat = chosen.reshape(QB * ATT * BLOCK, CH)
        obs_keys = project(flat, obs_key_weight).reshape(QB, ATT * BLOCK, HEADS, HDIM)
        obs_values = project(flat, obs_value_weight).reshape(QB, ATT * BLOCK, HEADS, HDIM)
        row_limit = jnp.take(obs_count, source_device)
        row_index = block_index[..., None] * BLOCK + jnp.arange(BLOCK, dtype=jnp.int32)[None, None, :]
        row_ok = (present[..., None] & (row_index < row_limit[..., None])).reshape(QB, ATT * BLOCK)
        all_keys = jnp.concatenate([jnp.broadcast_to(tile_keys[None], (QB,) + tile_keys.shape), obs_keys], axis=1)
        all_values = jnp.concatenate([jnp.broadcast_to(tile_values[None], (QB,) + tile_values.shape), obs_values], axis=1)
        allowed = jnp.concatenate([jnp.full((QB, latent_rows), True), row_ok], axis=1)
        scores = jnp.einsum('nqhe,nkhe->nhqk', queries.astype(jnp.float32), all_keys.astype(jnp.float32)) / math.sqrt(HDIM)
        capped = SOFT_LIMIT * jnp.tanh(scores / SOFT_LIMIT)
        weights = jnp.where(allowed[:, None, None, :], jnp.exp(capped), jnp.float32(0.0))
        totals = lax.optimization_barrier(jnp.sum(weights, axis=-1))
        rounded = weights.astype(jnp.bfloat16)
        mixture = jnp.einsum('nhqk,nkhe->nqhe', rounded.astype(jnp.float32), all_values.astype(jnp.float32))
        mixture = mixture / jnp.transpose(totals, (0, 2, 1))[..., None]
        mixture = mixture.reshape(Q_DEV, HEADS * HDIM)
        normed = (mixture * lax.rsqrt(lax.optimization_barrier(jnp.mean(mixture * mixture, axis=-1, keepdims=True)) + EPSILON)).astype(jnp.bfloat16)
        return (own_rows.astype(jnp.float32) + jnp.dot(normed, out_weight, preferred_element_type=jnp.float32)).astype(jnp.bfloat16)
    updated = lax.map(one_device, jnp.arange(N_TILE * N_GRP, dtype=jnp.int32))
    return updated.reshape(N_TILE * N_GRP * Q_DEV, HEADS * HDIM)
```

```python
import functools

import jax
import jax.numpy as jnp
from jax import lax
from jax.experimental import pallas as pl
from jax.experimental.pallas import tpu as pltpu
from jax.sharding import PartitionSpec as P

HEADS = 8
HDIM = 64
BLOCK = 128
WIDTH = 512
PAIRS = HEADS // 2
SOFT_LIMIT = 20.0
EPSILON = 1e-06
LOG2E = 1.4426950408889634
NZ, NX, NC, NG = 8, 4, 2, 4
SLOTS = NZ * NX * NC
DZ_ORDER = (4, 3, 5, 2, 6, 1, 7, 0)
MESH = pl.DeviceIdType.MESH
NT = (((1,), (1,)), ((), ()))


def f32dot(a, b):
    return jnp.dot(a, b, preferred_element_type=jnp.float32)


def f32dot_nt(a, b):
    return lax.dot_general(a, b, NT, preferred_element_type=jnp.float32)


def kernel(
    send_idx,
    valid_rows,
    query_pick,
    obs_ref,
    okw_ref,
    ovw_ref,
    bg_ref,
    qw_ref,
    kw_ref,
    vw_ref,
    ow_ref,
    out_ref,
    packed,
    recv,
    bgs,
    qbd,
    ovwt,
    vwt,
    acc,
    tot,
    send_sem,
    recv_sem,
    bsend_sem,
    brecv_sem,
):
    tile = lax.axis_index("tile")
    grp = lax.axis_index("grp")
    z, x, c = tile // (NX * NC), (tile // NC) % NX, tile % NC

    def shifted(dz, o, sign):
        dx, dc = o // NC, o % NC
        zz = (z + sign * dz + NZ) % NZ
        xx = (x + sign * dx + NX) % NX
        cc = (c + dc) % NC
        return (zz * NX + xx) * NC + cc

    barrier = pltpu.get_barrier_semaphore()

    def greet(i, carry):
        pl.semaphore_signal(barrier, inc=1, device_id=((tile + i) % SLOTS, grp), device_id_type=MESH)
        return carry

    lax.fori_loop(1, SLOTS, greet, 0)
    for i in range(1, NG):
        pl.semaphore_signal(barrier, inc=1, device_id=(tile, (grp + i) % NG), device_id_type=MESH)
    pl.semaphore_wait(barrier, SLOTS - 1 + NG - 1)

    def slot_copy(i, dest):
        return pltpu.make_async_remote_copy(
            src_ref=packed.at[i],
            dst_ref=recv.at[i],
            send_sem=send_sem.at[i],
            recv_sem=recv_sem.at[i],
            device_id=(dest, grp),
            device_id_type=MESH,
        )

    def bg_copy(i):
        return pltpu.make_async_remote_copy(
            src_ref=bg_ref,
            dst_ref=bgs.at[i - 1],
            send_sem=bsend_sem.at[i - 1],
            recv_sem=brecv_sem.at[i - 1],
            device_id=(tile, (grp + i) % NG),
            device_id_type=MESH,
        )

    for i in range(1, NG):
        bg_copy(i).start()

    def send_round(o, carry):
        for pos, dz in enumerate(DZ_ORDER):
            i = o * NZ + pos
            dest = shifted(dz, o, 1)
            block = obs_ref[send_idx[dest]]
            if dz == 0:

                @pl.when(o == 0)
                def _():
                    recv[i] = block

                @pl.when(o > 0)
                def _():
                    packed[i] = block
                    slot_copy(i, dest).start()

            else:
                packed[i] = block
                slot_copy(i, dest).start()
        return carry

    lax.fori_loop(0, NX * NC, send_round, 0)

    ovwt[...] = ovw_ref[...].T
    vwt[...] = vw_ref[...].T
    qwt = qw_ref[...].T
    qt = f32dot_nt(qwt, bg_ref[...]).astype(jnp.bfloat16)
    qbd[...] = jnp.zeros_like(qbd)
    for b in range(2):
        for h in range(HEADS):
            half = h % 2
            qbd[b, h // 2, half * HDIM : (half + 1) * HDIM, half * BLOCK : (half + 1) * BLOCK] = qt[
                h * HDIM : (h + 1) * HDIM, b * BLOCK : (b + 1) * BLOCK
            ]
    acc[...] = jnp.zeros_like(acc)
    tot[...] = jnp.zeros_like(tot)

    def weigh(keys, p, pick):
        s = f32dot(keys[:, p * 2 * HDIM : (p + 1) * 2 * HDIM], qbd[pick, p])
        capped = jnp.tanh(s * (1.0 / (8.0 * SOFT_LIMIT)))
        return jnp.exp2(capped * (SOFT_LIMIT * LOG2E)).astype(jnp.bfloat16)

    def attend(keys, vt, mask_rows, p, pick):
        w = weigh(keys, p, pick)
        va = jnp.concatenate([vt[p * 2 * HDIM : (p + 1) * 2 * HDIM], mask_rows], axis=0)
        o = f32dot(va, w)
        return o[:HDIM, :BLOCK], o[HDIM : 2 * HDIM, BLOCK:], o[2 * HDIM : 2 * HDIM + 8]

    ones = jnp.ones((16, BLOCK), jnp.bfloat16)

    def latent_block(rows):
        keys = f32dot(rows, kw_ref[...]).astype(jnp.bfloat16)
        vt = f32dot_nt(vwt[...], rows).astype(jnp.bfloat16)
        for b in range(2):
            for p in range(PAIRS):
                top, low, total = attend(keys, vt, ones, p, b)
                acc[b, 2 * p] += top
                acc[b, 2 * p + 1] += low
                tot[b, p] += total

    def own_latents(j, carry):
        latent_block(bg_ref[pl.ds(pl.multiple_of(j * BLOCK, BLOCK), BLOCK), :])
        return carry

    lax.fori_loop(0, 2, own_latents, 0)

    def slot_step(i, carry):
        o, pos = i // NZ, i % NZ
        dz = jnp.where(pos == 0, 4, jnp.where(pos == 7, 0, jnp.where(pos % 2 == 1, 4 - (pos + 1) // 2, 4 + pos // 2)))
        source = shifted(dz, o, -1)

        @pl.when(i != NZ - 1)
        def _():
            slot_copy(i, tile).wait_recv()

        rows_ok = valid_rows[source]
        pick = query_pick[source]
        row_id = lax.broadcasted_iota(jnp.int32, (BLOCK, obs_ref.shape[2]), 0)
        block = recv[i]
        block = jnp.where(row_id < rows_ok, block, jnp.zeros_like(block))
        lane_id = lax.broadcasted_iota(jnp.int32, (16, BLOCK), 1)
        mask_rows = jnp.where(lane_id < rows_ok, 1.0, 0.0).astype(jnp.bfloat16)
        keys = f32dot(block, okw_ref[...]).astype(jnp.bfloat16)
        vt = f32dot_nt(ovwt[...], block).astype(jnp.bfloat16)
        first = pick == 0
        for p in range(PAIRS):
            top, low, total = attend(keys, vt, mask_rows, p, pick)
            for b in range(2):
                mine = first if b == 0 else jnp.logical_not(first)
                acc[b, 2 * p] += jnp.where(mine, top, 0.0)
                acc[b, 2 * p + 1] += jnp.where(mine, low, 0.0)
                tot[b, p] += jnp.where(mine, total, 0.0)
        return carry

    lax.fori_loop(0, NZ, slot_step, 0)
    for i in range(1, NG):
        bg_copy(i).wait_recv()

        def other_latents(j, carry, i=i):
            latent_block(bgs[i - 1, pl.ds(pl.multiple_of(j * BLOCK, BLOCK), BLOCK), :])
            return carry

        lax.fori_loop(0, 2, other_latents, 0)
    lax.fori_loop(NZ, SLOTS, slot_step, 0)

    for b in range(2):
        parts = []
        for h in range(HEADS):
            total = tot[b, h // 2, 0:1, (h % 2) * BLOCK : (h % 2 + 1) * BLOCK]
            parts.append(acc[b, h] / total)
        mixture = jnp.concatenate(parts, axis=0)
        scale = lax.rsqrt(jnp.mean(mixture * mixture, axis=0, keepdims=True) + EPSILON)
        normed = (mixture * scale).T.astype(jnp.bfloat16)
        rows = slice(b * BLOCK, (b + 1) * BLOCK)
        out_ref[rows, :] = (bg_ref[rows, :].astype(jnp.float32) + f32dot(normed, ow_ref[...])).astype(jnp.bfloat16)

    def finish(i, carry):
        @pl.when(i != NZ - 1)
        def _():
            slot_copy(i, tile).wait_send()

        return carry

    lax.fori_loop(0, SLOTS, finish, 0)
    for i in range(1, NG):
        bg_copy(i).wait_send()


def tables(owners, attend_list, obs_count):
    tile = lax.axis_index("tile")
    grp = lax.axis_index("grp")
    tiles = jnp.arange(SLOTS, dtype=jnp.int32)
    by_group = lax.dynamic_index_in_dim(owners.reshape(SLOTS, NG, -1), grp, 1, keepdims=False)
    counts = lax.dynamic_index_in_dim(obs_count.reshape(SLOTS, NG), grp, 1, keepdims=False)
    mine = lax.dynamic_index_in_dim(by_group, tile, 0, keepdims=False)
    blocks = jnp.arange(mine.shape[0], dtype=jnp.int32)
    send_idx = jnp.sum(jnp.where(mine[None, :] == tiles[:, None], blocks[None, :], 0), axis=1)
    owned = by_group == tile
    limits = jnp.clip(counts[:, None] - blocks[None, :] * BLOCK, 0, BLOCK)
    valid_rows = jnp.sum(jnp.where(owned, limits, 0), axis=1)
    query_pick = jnp.max((attend_list[1][None, :] == tiles[:, None]).astype(jnp.int32), axis=1)
    return send_idx, valid_rows, query_pick


def local(
    observations,
    obs_key_weight,
    obs_value_weight,
    background,
    query_weight,
    key_weight,
    value_weight,
    out_weight,
    owners,
    attend_list,
    obs_count,
):
    send_idx, valid_rows, query_pick = tables(owners, attend_list, obs_count)
    channels = observations.shape[1]
    blocks = observations.reshape(-1, BLOCK, channels)
    smem = pl.BlockSpec(memory_space=pltpu.SMEM)
    vmem = pl.BlockSpec(memory_space=pltpu.VMEM)
    bf16, f32 = jnp.bfloat16, jnp.float32
    return pl.pallas_call(
        kernel,
        out_shape=jax.ShapeDtypeStruct(background.shape, bf16),
        in_specs=[smem] * 3 + [vmem] * 8,
        out_specs=vmem,
        scratch_shapes=[
            pltpu.VMEM((SLOTS, BLOCK, channels), bf16),
            pltpu.VMEM((SLOTS, BLOCK, channels), bf16),
            pltpu.VMEM((NG - 1, 2 * BLOCK, WIDTH), bf16),
            pltpu.VMEM((2, PAIRS, 2 * HDIM, 2 * BLOCK), bf16),
            pltpu.VMEM((WIDTH, channels), bf16),
            pltpu.VMEM((WIDTH, WIDTH), bf16),
            pltpu.VMEM((2, HEADS, HDIM, BLOCK), f32),
            pltpu.VMEM((2, PAIRS, 8, 2 * BLOCK), f32),
            pltpu.SemaphoreType.DMA((SLOTS,)),
            pltpu.SemaphoreType.DMA((SLOTS,)),
            pltpu.SemaphoreType.DMA((NG - 1,)),
            pltpu.SemaphoreType.DMA((NG - 1,)),
        ],
        compiler_params=pltpu.CompilerParams(
            collective_id=0, has_side_effects=True, vmem_limit_bytes=40 * 1024 * 1024
        ),
        cost_estimate=pl.CostEstimate(flops=12_000_000_000, bytes_accessed=8_000_000, transcendentals=21_000_000),
    )(
        send_idx,
        valid_rows,
        query_pick,
        blocks,
        obs_key_weight,
        obs_value_weight,
        background,
        query_weight,
        key_weight,
        value_weight,
        out_weight,
    )


def solution(mesh):
    rows = P(("tile", "grp"), None)
    in_specs = (rows, P(), P(), rows, P(), P(), P(), P(), P(), rows, P())
    return jax.shard_map(local, mesh=mesh, in_specs=in_specs, out_specs=rows, check_vma=False)
```

```python
import functools

import jax
import jax.numpy as jnp
from jax import lax
from jax.experimental import pallas as pl
from jax.experimental.pallas import tpu as pltpu
from jax.sharding import PartitionSpec as P

HEADS = 8
HDIM = 64
BLOCK = 128
WIDTH = 512
CHANNELS = 256
PAIRS = HEADS // 2
SOFT_LIMIT = 20.0
EPSILON = 1e-06
LOG2E = 1.4426950408889634
NZ, NX, NC, NG = 8, 4, 2, 4
SIDE = NX * NC
SLOTS = NZ * SIDE
RING = SLOTS * NG
STRIDE = RING // NZ
OBS_BLOCKS = 32
CHUNK = 4
CHUNKS = 10
TURNS = CHUNK * CHUNKS
LAG = 2 * CHUNK
BOUNDS = (20, 32, 40, 40)
MESH = pl.DeviceIdType.MESH
NT = (((1,), (1,)), ((), ()))


def relay_plan(owners, counts, second, tile, grp, roll):
    f32, i32 = jnp.float32, jnp.int32
    n_blk = owners.shape[0]
    z, x, c = tile // (NX * NC), (tile // NC) % NX, tile % NC
    me = tile * NG + grp
    lane = lax.broadcasted_iota(i32, (n_blk, RING), 1)
    block = lax.broadcasted_iota(i32, (n_blk, RING), 0)
    lane_row = lane[:1]

    def tally(cond):
        return jnp.sum(jnp.where(cond, 1.0, 0.0).astype(f32), axis=0, keepdims=True)

    def column(values, which):
        return jnp.sum(jnp.where(lane[: values.shape[0]] == which, values, 0.0), axis=1, keepdims=True)

    live = block * BLOCK < counts
    away = (owners // (NX * NC) - lane // STRIDE + NZ) % NZ
    side = (owners // NC) % NX
    core = owners % NC
    right = (away >= 1) & ((away < NZ // 2) | ((away == NZ // 2) & ((side + core) % 2 == 0)))
    left = (away >= NZ // 2) & jnp.logical_not(right)
    hops = jnp.where(right, away, jnp.where(left, NZ - away, 0))
    moving = live & (hops > 0)
    shift = (side - (lane // (NC * NG)) % NX + NX + NX - 1) % NX
    order = (4 - hops) * (NX * NC) + shift * NC + core + jnp.where(right, 0, 64)
    key = jnp.where(moving, order, 1000)
    rank = jnp.zeros((n_blk, RING), f32)
    for k in range(n_blk):
        other = key[k : k + 1]
        rank += jnp.where((other < key) & ((other < 64) == (key < 64)), 1.0, 0.0)
    ahead, starts, over = {}, {}, jnp.zeros((1, RING), f32)
    for d, way in enumerate((right, left)):
        turn = 1 if d == 0 else -1
        count = [tally(moving & way & (hops >= k)) for k in range(1, 5)]
        begin = [jnp.zeros((1, RING), f32)]
        for k in range(1, 4):
            length = roll(count[k - 1], turn * (k - 1) * STRIDE)
            begin.append(jnp.maximum(begin[-1] + length, roll(begin[-1], turn * STRIDE) + LAG))
        for k in range(4):
            length = roll(count[k], turn * k * STRIDE)
            over = jnp.maximum(over, begin[k] + length - BOUNDS[k])
            ahead[d, k] = length
            starts[d, k] = begin[k]
    spot = jnp.zeros((n_blk, RING), f32)
    for d, way in enumerate((right, left)):
        turn = 1 if d == 0 else -1
        for k in range(4):
            landed = roll(starts[d, k], -turn * k * STRIDE)
            spot = jnp.where(way & (hops == k + 1), landed + rank + (n_blk + d * TURNS), spot)
    blockf = block.astype(f32)
    spot = jnp.where(hops == 0, blockf, spot)
    spot = jnp.where(live, spot, -1.0)
    rows = []
    turns = lane_row.astype(f32)
    own_key, own_rank = column(key.astype(f32), me), column(rank, me)
    for d in range(2):
        turn = 1 if d == 0 else -1
        mine = (own_key < 64.0) if d == 0 else ((own_key >= 64.0) & (own_key < 1000.0))
        source = jnp.sum(jnp.where(mine & (own_rank == turns), blockf, 0.0), axis=0, keepdims=True)
        before = (me - turn * STRIDE + RING) % RING
        for k in range(1, 4):
            begin, length = column(starts[d, k], me), column(ahead[d, k], me)
            old = column(starts[d, k - 1], before)
            inside = (turns >= begin) & (turns < begin + length)
            source = jnp.where(inside, turns - begin + old + (n_blk + d * TURNS), source)
        rows.append(source)
    group = lane_row // (NX * NC)
    owner_cols = jnp.zeros((n_blk, RING), f32)
    spot_cols = jnp.zeros((n_blk, RING), f32)
    ownersf = owners.astype(f32)
    for g in range(NZ):
        dz = (g + 1) // 2 if g % 2 else (NZ - g // 2) % NZ
        origin = (me - dz * STRIDE + RING) % RING
        owner_cols = jnp.where(group == g, column(ownersf, origin), owner_cols)
        spot_cols = jnp.where(group == g, column(spot, origin), spot_cols)
    local = lane_row % (NX * NC)
    dest = (z * NX + (x + local // NC) % NX) * NC + (c + local % NC) % NC
    found = (owner_cols == dest.astype(f32)) & (spot_cols >= 0.0)
    rows.append(jnp.sum(jnp.where(found, spot_cols, 0.0), axis=0, keepdims=True))
    limits = jnp.clip(counts - block * BLOCK, 0, BLOCK).astype(f32)
    rows.append(jnp.sum(jnp.where(owners == tile, limits, 0.0), axis=0, keepdims=True))
    pick = jnp.zeros((1, RING), f32)
    for entry in second:
        pick = jnp.where(lane_row == entry, 1.0, pick)
    rows.append(pick)
    rows.append(jnp.broadcast_to(jnp.max(over, axis=1, keepdims=True), (1, RING)))
    own_owner = column(ownersf, me)
    rows.append(jnp.sum(jnp.where(own_owner == turns, blockf, 0.0), axis=0, keepdims=True))
    rows.append(jnp.zeros((1, RING), f32))
    return jnp.concatenate(rows, axis=0).astype(i32)


def plan_kernel(list_ref, owners_ref, counts_ref, out_ref):
    tile, grp = lax.axis_index("tile"), lax.axis_index("grp")
    second = [list_ref[1, k] for k in range(list_ref.shape[1])]
    out_ref[...] = relay_plan(
        owners_ref[...], counts_ref[...], second, tile, grp, lambda a, n: pltpu.roll(a, n % RING, 1)
    )


def f32dot(a, b):
    return jnp.dot(a, b, preferred_element_type=jnp.float32)


def f32dot_nt(a, b):
    return lax.dot_general(a, b, NT, preferred_element_type=jnp.float32)


class Parts:
    def __init__(self, table, hbm, out_ref, work):
        (self.obs, *self.sources) = hbm
        (self.recv, self.bgs, self.okw, self.ovw, self.qw, self.kw, self.vw, self.ow) = work[:8]
        (self.qbd, self.ovwt, self.vwt, self.acc, self.tot) = work[8:13]
        (self.load_sem, self.bsend_sem, self.brecv_sem) = work[13:]
        self.table, self.out_ref = table, out_ref
        self.tile, self.grp = lax.axis_index("tile"), lax.axis_index("grp")
        self.z, self.x, self.c = self.tile // SIDE, (self.tile // NC) % NX, self.tile % NC

    def at(self, dz, dx, dc):
        zz, xx, cc = (self.z + dz + NZ) % NZ, (self.x + dx + NX) % NX, (self.c + dc) % NC
        return (zz * NX + xx) * NC + cc

    def loads(self, obs_target):
        targets = (self.okw, self.ovw, self.bgs.at[0], self.qw, self.kw, self.vw, self.ow)
        pairs = [(self.obs, obs_target)] + list(zip(self.sources, targets))
        return [pltpu.make_async_copy(a, b, self.load_sem.at[k]) for k, (a, b) in enumerate(pairs)]

    def bg_copy(self, i):
        return pltpu.make_async_remote_copy(
            src_ref=self.bgs.at[0],
            dst_ref=self.bgs.at[i],
            send_sem=self.bsend_sem.at[i - 1],
            recv_sem=self.brecv_sem.at[i - 1],
            device_id=(self.tile, (self.grp + i) % NG),
            device_id_type=MESH,
        )

    def setup(self):
        self.ovwt[...] = self.ovw[...].T
        self.vwt[...] = self.vw[...].T
        qt = f32dot_nt(self.qw[...].T, self.bgs[0]).astype(jnp.bfloat16)
        self.qbd[...] = jnp.zeros_like(self.qbd)
        for b in range(2):
            for h in range(HEADS):
                half = h % 2
                rows, lanes = slice(half * HDIM, (half + 1) * HDIM), slice(half * BLOCK, (half + 1) * BLOCK)
                self.qbd[b, h // 2, rows, lanes] = qt[h * HDIM : (h + 1) * HDIM, b * BLOCK : (b + 1) * BLOCK]
        self.acc[...] = jnp.zeros_like(self.acc)
        self.tot[...] = jnp.zeros_like(self.tot)

    def attend(self, keys, vt, mask_rows, p, pick):
        s = f32dot(keys[:, p * 2 * HDIM : (p + 1) * 2 * HDIM], self.qbd[pick, p])
        capped = jnp.tanh(s * (1.0 / (8.0 * SOFT_LIMIT)))
        w = jnp.exp2(capped * (SOFT_LIMIT * LOG2E)).astype(jnp.bfloat16)
        va = jnp.concatenate([vt[p * 2 * HDIM : (p + 1) * 2 * HDIM], mask_rows], axis=0)
        o = f32dot(va, w)
        return o[:HDIM, :BLOCK], o[HDIM : 2 * HDIM, BLOCK:], o[2 * HDIM : 2 * HDIM + 8]

    def latent_step(self, j, carry):
        rows = self.bgs[j // 2, pl.ds(pl.multiple_of((j % 2) * BLOCK, BLOCK), BLOCK), :]
        keys = f32dot(rows, self.kw[...]).astype(jnp.bfloat16)
        vt = f32dot_nt(self.vwt[...], rows).astype(jnp.bfloat16)
        ones = jnp.ones((16, BLOCK), jnp.bfloat16)
        for b in range(2):
            for p in range(PAIRS):
                top, low, total = self.attend(keys, vt, ones, p, b)
                self.acc[b, 2 * p] += top
                self.acc[b, 2 * p + 1] += low
                self.tot[b, p] += total
        return carry

    def slot_way(self, i):
        g, o = i // SIDE, i % SIDE
        dz = jnp.where(g % 2 == 1, (g + 1) // 2, (NZ - g // 2) % NZ)
        return dz, o // NC, o % NC

    def slot_math(self, i):
        dz, dx, dc = self.slot_way(i)
        source = self.at(-dz, -dx, -dc)
        rows_ok = self.table[3, source * NG + self.grp]
        pick = self.table[4, source]
        row_id = lax.broadcasted_iota(jnp.int32, (BLOCK, CHANNELS), 0)
        block = self.recv[i]
        block = jnp.where(row_id < rows_ok, block, jnp.zeros_like(block))
        lane_id = lax.broadcasted_iota(jnp.int32, (16, BLOCK), 1)
        mask_rows = jnp.where(lane_id < rows_ok, 1.0, 0.0).astype(jnp.bfloat16)
        keys = f32dot(block, self.okw[...]).astype(jnp.bfloat16)
        vt = f32dot_nt(self.ovwt[...], block).astype(jnp.bfloat16)
        first = pick == 0
        for p in range(PAIRS):
            top, low, total = self.attend(keys, vt, mask_rows, p, pick)
            for b in range(2):
                mine = first if b == 0 else jnp.logical_not(first)
                self.acc[b, 2 * p] += jnp.where(mine, top, 0.0)
                self.acc[b, 2 * p + 1] += jnp.where(mine, low, 0.0)
                self.tot[b, p] += jnp.where(mine, total, 0.0)

    def result(self):
        for b in range(2):
            parts = []
            for h in range(HEADS):
                total = self.tot[b, h // 2, 0:1, (h % 2) * BLOCK : (h % 2 + 1) * BLOCK]
                parts.append(self.acc[b, h] / total)
            mixture = jnp.concatenate(parts, axis=0)
            scale = lax.rsqrt(jnp.mean(mixture * mixture, axis=0, keepdims=True) + EPSILON)
            normed = (mixture * scale).T.astype(jnp.bfloat16)
            rows = slice(b * BLOCK, (b + 1) * BLOCK)
            update = f32dot(normed, self.ow[...])
            self.out_ref[rows, :] = (self.bgs[0, rows, :].astype(jnp.float32) + update).astype(jnp.bfloat16)


def slot_copier(me, packed, send_sem, recv_sem):
    def slot_copy(i, dest):
        return pltpu.make_async_remote_copy(
            src_ref=packed.at[i],
            dst_ref=me.recv.at[i],
            send_sem=send_sem.at[i],
            recv_sem=recv_sem.at[i],
            device_id=(dest, me.grp),
            device_id_type=MESH,
        )

    return slot_copy


def direct_kernel(table, *refs):
    hbm, out_ref, (held, packed, send_sem, recv_sem), work = refs[:8], refs[8], refs[9:13], refs[13:]
    me = Parts(table, hbm, out_ref, work)
    loads = me.loads(held)
    for load in loads:
        load.start()
    barrier = pltpu.get_barrier_semaphore()

    def greet(i, carry):
        pl.semaphore_signal(barrier, inc=1, device_id=((me.tile + i) % SLOTS, me.grp), device_id_type=MESH)
        return carry

    lax.fori_loop(1, SLOTS, greet, 0)
    for i in range(1, NG):
        pl.semaphore_signal(barrier, inc=1, device_id=(me.tile, (me.grp + i) % NG), device_id_type=MESH)
    for load in loads:
        load.wait()
    pl.semaphore_wait(barrier, SLOTS - 1 + NG - 1)
    slot_copy = slot_copier(me, packed, send_sem, recv_sem)
    for i in range(1, NG):
        me.bg_copy(i).start()

    def send(n, carry):
        i = (n % NZ) * SIDE + n // NZ
        dest = me.at(*me.slot_way(i))
        block = held[table[6, dest]]

        @pl.when(i == 0)
        def _():
            me.recv[i] = block

        @pl.when(i > 0)
        def _():
            packed[i] = block
            slot_copy(i, dest).start()

        return carry

    lax.fori_loop(0, SLOTS, send, 0)
    me.setup()
    for i in range(1, NG):
        me.bg_copy(i).wait_recv()
    lax.fori_loop(0, 2 * NG, me.latent_step, 0)

    def step(n, carry):
        i = (n % NZ) * SIDE + n // NZ

        @pl.when(i > 0)
        def _():
            slot_copy(i, me.tile).wait_recv()

        me.slot_math(i)
        return carry

    lax.fori_loop(0, SLOTS, step, 0)
    me.result()

    def finish(i, carry):
        slot_copy(i, me.tile).wait_send()
        return carry

    lax.fori_loop(1, SLOTS, finish, 0)
    for i in range(1, NG):
        me.bg_copy(i).wait_send()


def pick_step(m, table):
    value = table[-1]
    for k in range(len(table) - 2, -1, -1):
        value = jnp.where(m == k, table[k], value)
    return value


LATENTS_BY = (0, 0, 2, 4, 6, 8, 8, 8, 8, 8, 8, 8, 8)
SLOTS_BY = (0, 0, 0, 0, 2, 4, 8, 8, 16, 20, 24, 24)
GROUPS_BY = (1, 1, 1, 1, 1, 1, 3, 3, 3, 5, 5, 8)


def relay_kernel(table, *refs):
    hbm, out_ref = refs[:8], refs[8]
    (held, leaving, landing, packed, send_sem, recv_sem, zsend_sem, zrecv_sem), work = refs[9:17], refs[17:]
    me = Parts(table, hbm, out_ref, work)
    loads = me.loads(held.at[pl.ds(0, OBS_BLOCKS)])
    for load in loads:
        load.start()
    barrier = pltpu.get_barrier_semaphore()
    ring = (me.at(1, 0, 0), me.at(-1, 0, 0))
    peers = [(t, me.grp) for t in ring]
    peers += [(me.at(0, o // NC, o % NC), me.grp) for o in range(1, SIDE)]
    peers += [(me.tile, (me.grp + i) % NG) for i in range(1, NG)]
    for peer in peers:
        pl.semaphore_signal(barrier, inc=1, device_id=peer, device_id_type=MESH)
    loads[0].wait()
    pl.semaphore_wait(barrier, len(peers))
    slot_copy = slot_copier(me, packed, send_sem, recv_sem)

    def ring_copy(d, m):
        return pltpu.make_async_remote_copy(
            src_ref=leaving.at[d, m],
            dst_ref=landing.at[d, m],
            send_sem=zsend_sem.at[d, m],
            recv_sem=zrecv_sem.at[d, m],
            device_id=(ring[d], me.grp),
            device_id_type=MESH,
        )

    def side_send(i, carry):
        block = held[table[2, i]]
        o = i % SIDE

        @pl.when(o == 0)
        def _():
            me.recv[i] = block

        @pl.when(o > 0)
        def _():
            packed[i] = block
            slot_copy(i, me.at(0, o // NC, o % NC)).start()

        return carry

    def slot_step(i, carry):
        @pl.when(i % SIDE > 0)
        def _():
            slot_copy(i, me.tile).wait_recv()

        me.slot_math(i)
        return carry

    def step(m, carry):
        @pl.when(m >= 2)
        def _():
            for d in range(2):
                ring_copy(d, m - 2).wait_recv()
                for k in range(CHUNK):
                    held[OBS_BLOCKS + d * TURNS + (m - 2) * CHUNK + k] = landing[d, m - 2, k]

        @pl.when(m < CHUNKS)
        def _():
            for d in range(2):
                for k in range(CHUNK):
                    leaving[d, m, k] = held[table[d, m * CHUNK + k]]
                ring_copy(d, m).start()

        lax.fori_loop(
            jnp.where(m == 0, 0, pick_step(m - 1, GROUPS_BY)) * SIDE, pick_step(m, GROUPS_BY) * SIDE, side_send, 0
        )

        @pl.when(m == 1)
        def _():
            for load in loads[1:]:
                load.wait()
            for i in range(1, NG):
                me.bg_copy(i).start()
            me.setup()

        @pl.when(m == 3)
        def _():
            for i in range(1, NG):
                me.bg_copy(i).wait_recv()

        lax.fori_loop(jnp.where(m == 0, 0, pick_step(m - 1, LATENTS_BY)), pick_step(m, LATENTS_BY), me.latent_step, 0)
        lax.fori_loop(jnp.where(m == 0, 0, pick_step(m - 1, SLOTS_BY)), pick_step(m, SLOTS_BY), slot_step, 0)
        return carry

    lax.fori_loop(0, CHUNKS + 2, step, 0)
    lax.fori_loop(SLOTS_BY[-1], SLOTS, slot_step, 0)
    me.result()

    def finish(i, carry):
        @pl.when(i % SIDE > 0)
        def _():
            slot_copy(i, me.tile).wait_send()

        return carry

    lax.fori_loop(0, SLOTS, finish, 0)

    def ring_finish(m, carry):
        for d in range(2):
            ring_copy(d, m).wait_send()
        return carry

    lax.fori_loop(0, CHUNKS, ring_finish, 0)
    for i in range(1, NG):
        me.bg_copy(i).wait_send()


def exchange_call(kernel, collective_id, own_scratch, name):
    bf16, f32 = jnp.bfloat16, jnp.float32
    smem = pl.BlockSpec(memory_space=pltpu.SMEM)
    vmem = pl.BlockSpec(memory_space=pltpu.VMEM)
    hbm = pl.BlockSpec(memory_space=pl.ANY)
    shared = [
        pltpu.VMEM((SLOTS, BLOCK, CHANNELS), bf16),
        pltpu.VMEM((NG, 2 * BLOCK, WIDTH), bf16),
        pltpu.VMEM((CHANNELS, WIDTH), bf16),
        pltpu.VMEM((CHANNELS, WIDTH), bf16),
        pltpu.VMEM((WIDTH, WIDTH), bf16),
        pltpu.VMEM((WIDTH, WIDTH), bf16),
        pltpu.VMEM((WIDTH, WIDTH), bf16),
        pltpu.VMEM((WIDTH, WIDTH), bf16),
        pltpu.VMEM((2, PAIRS, 2 * HDIM, 2 * BLOCK), bf16),
        pltpu.VMEM((WIDTH, CHANNELS), bf16),
        pltpu.VMEM((WIDTH, WIDTH), bf16),
        pltpu.VMEM((2, HEADS, HDIM, BLOCK), f32),
        pltpu.VMEM((2, PAIRS, 8, 2 * BLOCK), f32),
        pltpu.SemaphoreType.DMA((8,)),
        pltpu.SemaphoreType.DMA((NG - 1,)),
        pltpu.SemaphoreType.DMA((NG - 1,)),
    ]
    return pl.pallas_call(
        kernel,
        out_shape=jax.ShapeDtypeStruct((2 * BLOCK, WIDTH), bf16),
        in_specs=[smem] + [hbm] * 8,
        out_specs=vmem,
        scratch_shapes=own_scratch + shared,
        compiler_params=pltpu.CompilerParams(
            collective_id=collective_id, has_side_effects=True, vmem_limit_bytes=48 * 1024 * 1024
        ),
        cost_estimate=pl.CostEstimate(flops=12_000_000_000, bytes_accessed=8_000_000, transcendentals=21_000_000),
        name=name,
    )


def slots_of(count):
    return pltpu.VMEM((count, BLOCK, CHANNELS), jnp.bfloat16)


def local(
    observations,
    obs_key_weight,
    obs_value_weight,
    background,
    query_weight,
    key_weight,
    value_weight,
    out_weight,
    owners,
    attend_list,
    obs_count,
):
    vmem = pl.BlockSpec(memory_space=pltpu.VMEM)
    table = pl.pallas_call(
        plan_kernel,
        out_shape=jax.ShapeDtypeStruct((8, RING), jnp.int32),
        in_specs=[pl.BlockSpec(memory_space=pltpu.SMEM), vmem, vmem],
        out_specs=vmem,
        name="plan",
    )(attend_list, owners.T, obs_count[None, :])
    dma = pltpu.SemaphoreType.DMA
    relay = exchange_call(
        relay_kernel,
        0,
        [
            slots_of(OBS_BLOCKS + 2 * TURNS),
            pltpu.VMEM((2, CHUNKS, CHUNK, BLOCK, CHANNELS), jnp.bfloat16),
            pltpu.VMEM((2, CHUNKS, CHUNK, BLOCK, CHANNELS), jnp.bfloat16),
            slots_of(SLOTS),
            dma((SLOTS,)),
            dma((SLOTS,)),
            dma((2, CHUNKS)),
            dma((2, CHUNKS)),
        ],
        "relay",
    )
    direct = exchange_call(
        direct_kernel, 1, [slots_of(OBS_BLOCKS), slots_of(SLOTS), dma((SLOTS,)), dma((SLOTS,))], "direct"
    )
    operands = (
        table,
        observations.reshape(OBS_BLOCKS, BLOCK, CHANNELS),
        obs_key_weight,
        obs_value_weight,
        background,
        query_weight,
        key_weight,
        value_weight,
        out_weight,
    )
    return lax.cond(table[5, 0] <= 0, lambda *a: relay(*a), lambda *a: direct(*a), *operands)


def solution(mesh):
    rows = P(("tile", "grp"), None)
    in_specs = (rows, P(), P(), rows, P(), P(), P(), P(), P(), rows, P())
    return jax.shard_map(local, mesh=mesh, in_specs=in_specs, out_specs=rows, check_vma=False)
```

```python
import functools

import jax
import jax.numpy as jnp
from jax import lax
from jax.experimental import pallas as pl
from jax.experimental.pallas import tpu as pltpu
from jax.sharding import PartitionSpec as P

HEADS = 8
HDIM = 64
BLOCK = 128
WIDTH = 512
CHANNELS = 256
PAIRS = HEADS // 2
SOFT_LIMIT = 20.0
EPSILON = 1e-06
LOG2E = 1.4426950408889634
NZ, NX, NC, NG = 8, 4, 2, 4
SIDE = NX * NC
SLOTS = NZ * SIDE
RING = SLOTS * NG
STRIDE = RING // NZ
OBS_BLOCKS = 32
CHUNK = 2
CHUNKS = 20
BEHIND = 3
TURNS = CHUNK * CHUNKS
LAG = BEHIND * CHUNK
BOUNDS = (20, 30, 38, 40)
BATCH = 4
MESH = pl.DeviceIdType.MESH
NT = (((1,), (1,)), ((), ()))


def relay_plan(owners, counts, second, tile, grp, roll):
    f32, i32 = jnp.float32, jnp.int32
    n_blk = owners.shape[0]
    z, x, c = tile // (NX * NC), (tile // NC) % NX, tile % NC
    me = tile * NG + grp
    lane = lax.broadcasted_iota(i32, (n_blk, RING), 1)
    block = lax.broadcasted_iota(i32, (n_blk, RING), 0)
    lane_row = lane[:1]

    def tally(cond):
        return jnp.sum(jnp.where(cond, 1.0, 0.0).astype(f32), axis=0, keepdims=True)

    def column(values, which):
        return jnp.sum(jnp.where(lane[: values.shape[0]] == which, values, 0.0), axis=1, keepdims=True)

    live = block * BLOCK < counts
    away = (owners // (NX * NC) - lane // STRIDE + NZ) % NZ
    side = (owners // NC) % NX
    core = owners % NC
    half = NZ // 2
    middle = live & (away == half)
    spare = tally(live & (away > half)) - tally(live & (away >= 1) & (away < half)) + tally(middle)
    share = jnp.floor((spare + (lane_row % 2).astype(f32)) * 0.5)
    seat, taken = side * NC + core, jnp.zeros((1, RING), f32)
    earlier = jnp.zeros((n_blk, RING), f32)
    for k in range(NX * NC):
        earlier = jnp.where(seat == k, taken, earlier)
        taken += tally(middle & (seat == k))
    right = (away >= 1) & ((away < half) | ((away == half) & (earlier < share)))
    left = (away >= NZ // 2) & jnp.logical_not(right)
    hops = jnp.where(right, away, jnp.where(left, NZ - away, 0))
    moving = live & (hops > 0)
    shift = (side - (lane // (NC * NG)) % NX + NX + NX - 1) % NX
    order = (4 - hops) * (NX * NC) + shift * NC + core + jnp.where(right, 0, 64)
    key = jnp.where(moving, order, 1000)
    rank = jnp.zeros((n_blk, RING), f32)
    for k in range(n_blk):
        other = key[k : k + 1]
        rank += jnp.where((other < key) & ((other < 64) == (key < 64)), 1.0, 0.0)
    ahead, starts, over = {}, {}, jnp.zeros((1, RING), f32)
    for d, way in enumerate((right, left)):
        turn = 1 if d == 0 else -1
        count = [tally(moving & way & (hops >= k)) for k in range(1, 5)]
        begin = [jnp.zeros((1, RING), f32)]
        for k in range(1, 4):
            length = roll(count[k - 1], turn * (k - 1) * STRIDE)
            begin.append(jnp.maximum(begin[-1] + length, roll(begin[-1], turn * STRIDE) + LAG))
        for k in range(4):
            length = roll(count[k], turn * k * STRIDE)
            over = jnp.maximum(over, begin[k] + length - BOUNDS[k])
            ahead[d, k] = length
            starts[d, k] = begin[k]
    spot = jnp.zeros((n_blk, RING), f32)
    for d, way in enumerate((right, left)):
        turn = 1 if d == 0 else -1
        for k in range(4):
            landed = roll(starts[d, k], -turn * k * STRIDE)
            spot = jnp.where(way & (hops == k + 1), landed + rank + (n_blk + d * TURNS), spot)
    blockf = block.astype(f32)
    spot = jnp.where(hops == 0, blockf, spot)
    spot = jnp.where(live, spot, -1.0)
    rows = []
    turns = lane_row.astype(f32)
    own_key, own_rank = column(key.astype(f32), me), column(rank, me)
    for d in range(2):
        turn = 1 if d == 0 else -1
        mine = (own_key < 64.0) if d == 0 else ((own_key >= 64.0) & (own_key < 1000.0))
        source = jnp.sum(jnp.where(mine & (own_rank == turns), blockf, 0.0), axis=0, keepdims=True)
        before = (me - turn * STRIDE + RING) % RING
        for k in range(1, 4):
            begin, length = column(starts[d, k], me), column(ahead[d, k], me)
            old = column(starts[d, k - 1], before)
            inside = (turns >= begin) & (turns < begin + length)
            source = jnp.where(inside, turns - begin + old + (n_blk + d * TURNS), source)
        rows.append(source)
    group = lane_row // (NX * NC)
    owner_cols = jnp.zeros((n_blk, RING), f32)
    spot_cols = jnp.zeros((n_blk, RING), f32)
    ownersf = owners.astype(f32)
    for g in range(NZ):
        dz = (g + 1) // 2 if g % 2 else (NZ - g // 2) % NZ
        origin = (me - dz * STRIDE + RING) % RING
        owner_cols = jnp.where(group == g, column(ownersf, origin), owner_cols)
        spot_cols = jnp.where(group == g, column(spot, origin), spot_cols)
    local = lane_row % (NX * NC)
    dest = (z * NX + (x + local // NC) % NX) * NC + (c + local % NC) % NC
    found = (owner_cols == dest.astype(f32)) & (spot_cols >= 0.0)
    rows.append(jnp.sum(jnp.where(found, spot_cols, 0.0), axis=0, keepdims=True))
    limits = jnp.clip(counts - block * BLOCK, 0, BLOCK).astype(f32)
    rows.append(jnp.sum(jnp.where(owners == tile, limits, 0.0), axis=0, keepdims=True))
    pick = jnp.zeros((1, RING), f32)
    for entry in second:
        pick = jnp.where(lane_row == entry, 1.0, pick)
    rows.append(pick)
    rows.append(jnp.broadcast_to(jnp.max(over, axis=1, keepdims=True), (1, RING)))
    own_owner = column(ownersf, me)
    rows.append(jnp.sum(jnp.where(own_owner == turns, blockf, 0.0), axis=0, keepdims=True))
    rows.append(jnp.zeros((1, RING), f32))
    return jnp.concatenate(rows, axis=0).astype(i32)


def plan_kernel(list_ref, owners_ref, counts_ref, out_ref):
    tile, grp = lax.axis_index("tile"), lax.axis_index("grp")
    second = [list_ref[1, k] for k in range(list_ref.shape[1])]
    out_ref[...] = relay_plan(
        owners_ref[...], counts_ref[...], second, tile, grp, lambda a, n: pltpu.roll(a, n % RING, 1)
    )


def f32dot(a, b):
    return jnp.dot(a, b, preferred_element_type=jnp.float32)


def f32dot_nt(a, b):
    return lax.dot_general(a, b, NT, preferred_element_type=jnp.float32)


class Parts:
    def __init__(self, table, hbm, out_ref, work):
        (self.obs, *self.sources) = hbm
        (self.recv, self.bgs, self.okw, self.ovw, self.qw, self.kw, self.vw, self.ow) = work[:8]
        (self.qbd, self.ovwt, self.vwt, self.acc, self.tot) = work[8:13]
        (self.load_sem, self.bsend_sem, self.brecv_sem) = work[13:]
        self.table, self.out_ref = table, out_ref
        self.tile, self.grp = lax.axis_index("tile"), lax.axis_index("grp")
        self.z, self.x, self.c = self.tile // SIDE, (self.tile // NC) % NX, self.tile % NC

    def at(self, dz, dx, dc):
        zz, xx, cc = (self.z + dz + NZ) % NZ, (self.x + dx + NX) % NX, (self.c + dc) % NC
        return (zz * NX + xx) * NC + cc

    def loads(self, obs_target):
        targets = (self.okw, self.ovw, self.bgs.at[0], self.qw, self.kw, self.vw, self.ow)
        pairs = [(self.obs, obs_target)] + list(zip(self.sources, targets))
        return [pltpu.make_async_copy(a, b, self.load_sem.at[k]) for k, (a, b) in enumerate(pairs)]

    def bg_copy(self, i):
        return pltpu.make_async_remote_copy(
            src_ref=self.bgs.at[0],
            dst_ref=self.bgs.at[i],
            send_sem=self.bsend_sem.at[i - 1],
            recv_sem=self.brecv_sem.at[i - 1],
            device_id=(self.tile, (self.grp + i) % NG),
            device_id_type=MESH,
        )

    def setup(self):
        self.ovwt[...] = self.ovw[...].T
        self.vwt[...] = self.vw[...].T
        qt = f32dot_nt(self.qw[...].T, self.bgs[0]).astype(jnp.bfloat16)
        self.qbd[...] = jnp.zeros_like(self.qbd)
        for b in range(2):
            for h in range(HEADS):
                half = h % 2
                rows, lanes = slice(half * HDIM, (half + 1) * HDIM), slice(half * BLOCK, (half + 1) * BLOCK)
                self.qbd[b, h // 2, rows, lanes] = qt[h * HDIM : (h + 1) * HDIM, b * BLOCK : (b + 1) * BLOCK]
        self.acc[...] = jnp.zeros_like(self.acc)
        self.tot[...] = jnp.zeros_like(self.tot)

    def weights(self, keys, p, pick):
        s = f32dot(keys[:, p * 2 * HDIM : (p + 1) * 2 * HDIM], self.qbd[pick, p])
        capped = jnp.tanh(s * (1.0 / (8.0 * SOFT_LIMIT)))
        return jnp.exp2(capped * (SOFT_LIMIT * LOG2E)).astype(jnp.bfloat16)

    def mix(self, vt, mask_rows, w, p):
        o = f32dot(jnp.concatenate([vt[p * 2 * HDIM : (p + 1) * 2 * HDIM], mask_rows], axis=0), w)
        return o[:HDIM, :BLOCK], o[HDIM : 2 * HDIM, BLOCK:], o[2 * HDIM : 2 * HDIM + 8]

    def add(self, b, p, terms):
        self.acc[b, 2 * p] += sum(t[0] for t in terms)
        self.acc[b, 2 * p + 1] += sum(t[1] for t in terms)
        self.tot[b, p] += sum(t[2] for t in terms)

    def latent_step(self, j, carry):
        rows = self.bgs[j]
        keys = f32dot(rows, self.kw[...]).astype(jnp.bfloat16)
        vt = f32dot_nt(self.vwt[...], rows).astype(jnp.bfloat16)
        ones = jnp.ones((16, 2 * BLOCK), jnp.bfloat16)
        ws = {(b, p): self.weights(keys, p, b) for p in range(PAIRS) for b in range(2)}
        for p in range(PAIRS):
            for b in range(2):
                self.add(b, p, [self.mix(vt, ones, ws[b, p], p)])
        return carry

    def slot_way(self, i):
        g, o = i // SIDE, i % SIDE
        dz = jnp.where(g % 2 == 1, (g + 1) // 2, (NZ - g // 2) % NZ)
        return dz, o // NC, o % NC

    def slot_math(self, first):
        picks, blocks, masks = [], [], []
        for k in range(BATCH):
            dz, dx, dc = self.slot_way(first + k)
            source = self.at(-dz, -dx, -dc)
            rows_ok = self.table[3, source * NG + self.grp]
            picks.append(self.table[4, source])
            row_id = lax.broadcasted_iota(jnp.int32, (BLOCK, CHANNELS), 0)
            block = self.recv[first + k]
            blocks.append(jnp.where(row_id < rows_ok, block, jnp.zeros_like(block)))
            lane_id = lax.broadcasted_iota(jnp.int32, (16, BLOCK), 1)
            masks.append(jnp.where(lane_id < rows_ok, 1.0, 0.0).astype(jnp.bfloat16))
        rows = jnp.concatenate(blocks, axis=0)
        keys = f32dot(rows, self.okw[...]).astype(jnp.bfloat16)
        vt = f32dot_nt(self.ovwt[...], rows).astype(jnp.bfloat16)
        part = [slice(k * BLOCK, (k + 1) * BLOCK) for k in range(BATCH)]
        ws = {(p, k): self.weights(keys[part[k]], p, picks[k]) for p in range(PAIRS) for k in range(BATCH)}
        for p in range(PAIRS):
            terms = [self.mix(vt[:, part[k]], masks[k], ws[p, k], p) for k in range(BATCH)]
            for b in range(2):
                self.add(b, p, [[jnp.where(picks[k] == b, v, 0.0) for v in terms[k]] for k in range(BATCH)])

    def result(self):
        for b in range(2):
            parts = []
            for h in range(HEADS):
                total = self.tot[b, h // 2, 0:1, (h % 2) * BLOCK : (h % 2 + 1) * BLOCK]
                parts.append(self.acc[b, h] / total)
            mixture = jnp.concatenate(parts, axis=0)
            scale = lax.rsqrt(jnp.mean(mixture * mixture, axis=0, keepdims=True) + EPSILON)
            normed = (mixture * scale).T.astype(jnp.bfloat16)
            rows = slice(b * BLOCK, (b + 1) * BLOCK)
            update = f32dot(normed, self.ow[...])
            self.out_ref[rows, :] = (self.bgs[0, rows, :].astype(jnp.float32) + update).astype(jnp.bfloat16)


def slot_copier(me, packed, send_sem, recv_sem):
    def slot_copy(i, dest):
        return pltpu.make_async_remote_copy(
            src_ref=packed.at[i],
            dst_ref=me.recv.at[i],
            send_sem=send_sem.at[i],
            recv_sem=recv_sem.at[i],
            device_id=(dest, me.grp),
            device_id_type=MESH,
        )

    return slot_copy


def direct_kernel(table, *refs):
    hbm, out_ref, (held, packed, send_sem, recv_sem), work = refs[:8], refs[8], refs[9:13], refs[13:]
    me = Parts(table, hbm, out_ref, work)
    loads = me.loads(held)
    for load in loads:
        load.start()
    barrier = pltpu.get_barrier_semaphore()

    def greet(i, carry):
        pl.semaphore_signal(barrier, inc=1, device_id=((me.tile + i) % SLOTS, me.grp), device_id_type=MESH)
        return carry

    lax.fori_loop(1, SLOTS, greet, 0)
    for i in range(1, NG):
        pl.semaphore_signal(barrier, inc=1, device_id=(me.tile, (me.grp + i) % NG), device_id_type=MESH)
    for load in loads:
        load.wait()
    pl.semaphore_wait(barrier, SLOTS - 1 + NG - 1)
    slot_copy = slot_copier(me, packed, send_sem, recv_sem)
    for i in range(1, NG):
        me.bg_copy(i).start()

    def send(i, carry):
        dest = me.at(*me.slot_way(i))
        block = held[table[6, dest]]

        @pl.when(i == 0)
        def _():
            me.recv[i] = block

        @pl.when(i > 0)
        def _():
            packed[i] = block
            slot_copy(i, dest).start()

        return carry

    lax.fori_loop(0, SLOTS, send, 0)
    me.setup()
    for i in range(1, NG):
        me.bg_copy(i).wait_recv()
    lax.fori_loop(0, NG, me.latent_step, 0)

    def step(n, carry):
        for k in range(BATCH):

            @pl.when(n * BATCH + k > 0)
            def _():
                slot_copy(n * BATCH + k, me.tile).wait_recv()

        me.slot_math(n * BATCH)
        return carry

    lax.fori_loop(0, SLOTS // BATCH, step, 0)
    me.result()

    def finish(i, carry):
        slot_copy(i, me.tile).wait_send()
        return carry

    lax.fori_loop(1, SLOTS, finish, 0)
    for i in range(1, NG):
        me.bg_copy(i).wait_send()


def reached(m, marks):
    return sum(jnp.where(m >= mark, 1, 0) for mark in marks)


LATENT_MARKS = (3, 5, 6, 7)
BATCH_MARKS = (8, 9, 15, 16, 17, 18, 20)
GROUP_MARKS = (0, 12, 12, 17, 17, 21, 21, 22)


def relay_kernel(table, *refs):
    hbm, out_ref = refs[:8], refs[8]
    (held, leaving, landing, packed, send_sem, recv_sem, zsend_sem, zrecv_sem), work = refs[9:17], refs[17:]
    me = Parts(table, hbm, out_ref, work)
    loads = me.loads(held.at[pl.ds(0, OBS_BLOCKS)])
    for load in loads:
        load.start()
    barrier = pltpu.get_barrier_semaphore()
    ring = (me.at(1, 0, 0), me.at(-1, 0, 0))
    peers = [(t, me.grp) for t in ring]
    peers += [(me.at(0, o // NC, o % NC), me.grp) for o in range(1, SIDE)]
    peers += [(me.tile, (me.grp + i) % NG) for i in range(1, NG)]
    for peer in peers:
        pl.semaphore_signal(barrier, inc=1, device_id=peer, device_id_type=MESH)
    loads[0].wait()
    pl.semaphore_wait(barrier, len(peers))
    slot_copy = slot_copier(me, packed, send_sem, recv_sem)

    def ring_copy(d, m):
        return pltpu.make_async_remote_copy(
            src_ref=leaving.at[d, m],
            dst_ref=landing.at[d, m],
            send_sem=zsend_sem.at[d, m],
            recv_sem=zrecv_sem.at[d, m],
            device_id=(ring[d], me.grp),
            device_id_type=MESH,
        )

    def side_send(i, carry):
        block = held[table[2, i]]
        o = i % SIDE

        @pl.when(o == 0)
        def _():
            me.recv[i] = block

        @pl.when(o > 0)
        def _():
            packed[i] = block
            slot_copy(i, me.at(0, o // NC, o % NC)).start()

        return carry

    def slot_step(n, carry):
        for k in range(BATCH):

            @pl.when((n * BATCH + k) % SIDE > 0)
            def _():
                slot_copy(n * BATCH + k, me.tile).wait_recv()

        me.slot_math(n * BATCH)
        return carry

    def step(m, carry):
        @pl.when(m >= BEHIND)
        def _():
            for d in range(2):
                ring_copy(d, m - BEHIND).wait_recv()
                for k in range(CHUNK):
                    held[OBS_BLOCKS + d * TURNS + (m - BEHIND) * CHUNK + k] = landing[d, m - BEHIND, k]

        @pl.when(m < CHUNKS)
        def _():
            for d in range(2):
                for k in range(CHUNK):
                    leaving[d, m, k] = held[table[d, m * CHUNK + k]]
                ring_copy(d, m).start()

        lax.fori_loop(reached(m - 1, GROUP_MARKS) * SIDE, reached(m, GROUP_MARKS) * SIDE, side_send, 0)

        @pl.when(m == 1)
        def _():
            for load in loads[1:]:
                load.wait()
            for i in range(1, NG):
                me.bg_copy(i).start()
            me.setup()

        @pl.when(m == LATENT_MARKS[1])
        def _():
            for i in range(1, NG):
                me.bg_copy(i).wait_recv()

        lax.fori_loop(reached(m - 1, LATENT_MARKS), reached(m, LATENT_MARKS), me.latent_step, 0)
        lax.fori_loop(reached(m - 1, BATCH_MARKS), reached(m, BATCH_MARKS), slot_step, 0)
        return carry

    lax.fori_loop(0, CHUNKS + BEHIND, step, 0)
    lax.fori_loop(len(BATCH_MARKS), SLOTS // BATCH, slot_step, 0)
    me.result()

    def finish(i, carry):
        @pl.when(i % SIDE > 0)
        def _():
            slot_copy(i, me.tile).wait_send()

        return carry

    lax.fori_loop(0, SLOTS, finish, 0)

    def ring_finish(m, carry):
        for d in range(2):
            ring_copy(d, m).wait_send()
        return carry

    lax.fori_loop(0, CHUNKS, ring_finish, 0)
    for i in range(1, NG):
        me.bg_copy(i).wait_send()


def exchange_call(kernel, collective_id, own_scratch, name):
    bf16, f32 = jnp.bfloat16, jnp.float32
    smem = pl.BlockSpec(memory_space=pltpu.SMEM)
    vmem = pl.BlockSpec(memory_space=pltpu.VMEM)
    hbm = pl.BlockSpec(memory_space=pl.ANY)
    shared = [
        pltpu.VMEM((SLOTS, BLOCK, CHANNELS), bf16),
        pltpu.VMEM((NG, 2 * BLOCK, WIDTH), bf16),
        pltpu.VMEM((CHANNELS, WIDTH), bf16),
        pltpu.VMEM((CHANNELS, WIDTH), bf16),
        pltpu.VMEM((WIDTH, WIDTH), bf16),
        pltpu.VMEM((WIDTH, WIDTH), bf16),
        pltpu.VMEM((WIDTH, WIDTH), bf16),
        pltpu.VMEM((WIDTH, WIDTH), bf16),
        pltpu.VMEM((2, PAIRS, 2 * HDIM, 2 * BLOCK), bf16),
        pltpu.VMEM((WIDTH, CHANNELS), bf16),
        pltpu.VMEM((WIDTH, WIDTH), bf16),
        pltpu.VMEM((2, HEADS, HDIM, BLOCK), f32),
        pltpu.VMEM((2, PAIRS, 8, 2 * BLOCK), f32),
        pltpu.SemaphoreType.DMA((8,)),
        pltpu.SemaphoreType.DMA((NG - 1,)),
        pltpu.SemaphoreType.DMA((NG - 1,)),
    ]
    return pl.pallas_call(
        kernel,
        out_shape=jax.ShapeDtypeStruct((2 * BLOCK, WIDTH), bf16),
        in_specs=[smem] + [hbm] * 8,
        out_specs=vmem,
        scratch_shapes=own_scratch + shared,
        compiler_params=pltpu.CompilerParams(
            collective_id=collective_id, has_side_effects=True, vmem_limit_bytes=48 * 1024 * 1024
        ),
        cost_estimate=pl.CostEstimate(flops=12_000_000_000, bytes_accessed=8_000_000, transcendentals=21_000_000),
        name=name,
    )


def slots_of(count):
    return pltpu.VMEM((count, BLOCK, CHANNELS), jnp.bfloat16)


def local(
    observations,
    obs_key_weight,
    obs_value_weight,
    background,
    query_weight,
    key_weight,
    value_weight,
    out_weight,
    owners,
    attend_list,
    obs_count,
):
    vmem = pl.BlockSpec(memory_space=pltpu.VMEM)
    table = pl.pallas_call(
        plan_kernel,
        out_shape=jax.ShapeDtypeStruct((8, RING), jnp.int32),
        in_specs=[pl.BlockSpec(memory_space=pltpu.SMEM), vmem, vmem],
        out_specs=vmem,
        name="plan",
    )(attend_list, owners.T, obs_count[None, :])
    dma = pltpu.SemaphoreType.DMA
    relay = exchange_call(
        relay_kernel,
        0,
        [
            slots_of(OBS_BLOCKS + 2 * TURNS),
            pltpu.VMEM((2, CHUNKS, CHUNK, BLOCK, CHANNELS), jnp.bfloat16),
            pltpu.VMEM((2, CHUNKS, CHUNK, BLOCK, CHANNELS), jnp.bfloat16),
            slots_of(SLOTS),
            dma((SLOTS,)),
            dma((SLOTS,)),
            dma((2, CHUNKS)),
            dma((2, CHUNKS)),
        ],
        "relay",
    )
    direct = exchange_call(
        direct_kernel, 1, [slots_of(OBS_BLOCKS), slots_of(SLOTS), dma((SLOTS,)), dma((SLOTS,))], "direct"
    )
    operands = (
        table,
        observations.reshape(OBS_BLOCKS, BLOCK, CHANNELS),
        obs_key_weight,
        obs_value_weight,
        background,
        query_weight,
        key_weight,
        value_weight,
        out_weight,
    )
    return lax.cond(table[5, 0] <= 0, lambda *a: relay(*a), lambda *a: direct(*a), *operands)


def solution(mesh):
    rows = P(("tile", "grp"), None)
    in_specs = (rows, P(), P(), rows, P(), P(), P(), P(), P(), rows, P())
    return jax.shard_map(local, mesh=mesh, in_specs=in_specs, out_specs=rows, check_vma=False)
```

```python
import functools

import jax
import jax.numpy as jnp
from jax import lax
from jax.experimental import pallas as pl
from jax.experimental.pallas import tpu as pltpu
from jax.sharding import PartitionSpec as P

HEADS = 8
HDIM = 64
BLOCK = 128
WIDTH = 512
CHANNELS = 256
PAIRS = HEADS // 2
SOFT_LIMIT = 20.0
EPSILON = 1e-06
LOG2E = 1.4426950408889634
NZ, NX, NC, NG = 8, 4, 2, 4
SIDE = NX * NC
SLOTS = NZ * SIDE
RING = SLOTS * NG
STRIDE = RING // NZ
OBS_BLOCKS = 32
CHUNK = 2
CHUNKS = 20
BEHIND = 3
TURNS = CHUNK * CHUNKS
LAG = BEHIND * CHUNK
FAR = 3
EARLY_DZ = (FAR, NZ - FAR)
EARLY = 4
EARLY_STEP = 6
ORDER = (("own", 1), ("early", 1), ("own", 2), ("early", 2), ("own", 3), ("early", 3), ("own", 4))
BOUNDS = {("own", 1): 18, ("own", 2): 28, ("own", 3): 36}
BATCH = 4
MESH = pl.DeviceIdType.MESH
NT = (((1,), (1,)), ((), ()))


def relay_plan(owners, counts, second, tile, grp, roll):
    f32, i32 = jnp.float32, jnp.int32
    n_blk = owners.shape[0]
    z, x, c = tile // (NX * NC), (tile // NC) % NX, tile % NC
    me = tile * NG + grp
    lane = lax.broadcasted_iota(i32, (n_blk, RING), 1)
    block = lax.broadcasted_iota(i32, (n_blk, RING), 0)
    lane_row = lane[:1]

    def tally(cond):
        return jnp.sum(jnp.where(cond, 1.0, 0.0).astype(f32), axis=0, keepdims=True)

    def column(values, which):
        return jnp.sum(jnp.where(lane[: values.shape[0]] == which, values, 0.0), axis=1, keepdims=True)

    live = block * BLOCK < counts
    away = (owners // (NX * NC) - lane // STRIDE + NZ) % NZ
    side = (owners // NC) % NX
    core = owners % NC
    half = NZ // 2
    ahead_of_z = (side - lane // (NC * NG) + 2 * NX) % NX == NX // 2
    early = ahead_of_z & ((away == FAR) | (away == NZ - FAR))
    going = live & (away > 0) & jnp.logical_not(early)
    middle = going & (away == half)
    spare = tally(going & (away > half)) - tally(going & (away < half)) + tally(middle)
    share = jnp.floor((spare + (lane_row % 2).astype(f32)) * 0.5)
    seat, taken = side * NC + core, jnp.zeros((1, RING), f32)
    earlier = jnp.zeros((n_blk, RING), f32)
    for k in range(NX * NC):
        earlier = jnp.where(seat == k, taken, earlier)
        taken += tally(middle & (seat == k))
    right = (away >= 1) & ((away < half) | ((away == half) & (earlier < share)))
    left = (away >= NZ // 2) & jnp.logical_not(right)
    hops = jnp.where(right, away, jnp.where(left, NZ - away, 0))
    moving = going
    shift = (side - (lane // (NC * NG)) % NX + NX + NX - 1) % NX
    order = (4 - hops) * (NX * NC) + shift * NC + core + jnp.where(right, 0, 64)
    key = jnp.where(moving, order, 1000)
    rank = jnp.zeros((n_blk, RING), f32)
    for k in range(n_blk):
        other = key[k : k + 1]
        rank += jnp.where((other < key) & ((other < 64) == (key < 64)), 1.0, 0.0)
    my_core = (lane_row // NG) % NC
    my_side = (lane_row // (NC * NG)) % NX
    hop_lanes = NC * NG * (NX // 2)

    def across(v):
        return jnp.where(my_side < NX // 2, roll(v, -hop_lanes), roll(v, hop_lanes))

    def sibling(v):
        return jnp.where(my_core == 0, roll(v, -NG), roll(v, NG))

    blockf = block.astype(f32)
    flag, early_idx = {}, []
    for dz in EARLY_DZ:
        sent = []
        for dest_core in range(NC):
            hit = live & early & (away == dz) & (core == dest_core)
            sent.append(across(tally(hit)))
            early_idx.append(jnp.sum(jnp.where(hit, blockf, 0.0), axis=0, keepdims=True))
        flag[dz, 0] = jnp.where(my_core == 0, sent[0], sent[1])
        flag[dz, 1] = jnp.where(my_core == 0, sibling(sent[0]), sibling(sent[1]))
    early_list = tuple(tuple((dz, dc) for dc in range(NC)) for dz in EARLY_DZ)
    lengths, starts, over = {}, {}, jnp.zeros((1, RING), f32)
    for d, way in enumerate((right, left)):
        turn = 1 if d == 0 else -1
        far = flag[early_list[d][0]] + flag[early_list[d][1]]
        position = jnp.zeros((1, RING), f32)
        for kind, k in ORDER:
            if kind == "own":
                count = tally(moving & way & (hops >= k))
            else:
                count = far
            length = roll(count, turn * (k - 1) * STRIDE)
            if k > 1:
                begin = jnp.maximum(position, roll(starts[d, kind, k - 1], turn * STRIDE) + LAG)
            else:
                begin = jnp.maximum(position, EARLY_STEP * CHUNK if kind == "early" else 0)
            position = jnp.where(length > 0, begin + length, position)
            over = jnp.maximum(over, position - BOUNDS.get((kind, k), TURNS))
            lengths[d, kind, k], starts[d, kind, k] = length, begin

    def landed(d, kind, k):
        return roll(starts[d, kind, k], (k if d else -k) * STRIDE + (STRIDE if d == 0 else -STRIDE))

    spot = jnp.zeros((n_blk, RING), f32)
    for d, way in enumerate((right, left)):
        for k in range(1, 5):
            spot = jnp.where(way & (hops == k), landed(d, "own", k) + rank + (n_blk + d * TURNS), spot)
    spot = jnp.where(hops == 0, blockf, spot)
    spot = jnp.where(live & jnp.logical_not(early), spot, -1.0)
    early_spot, first_early = {}, n_blk + 2 * TURNS
    own_early = []
    for d in range(2):
        before = jnp.zeros((1, RING), f32)
        chosen = []
        for dz, dc in early_list[d]:
            early_spot[dz, dc] = landed(d, "early", FAR) + before + (n_blk + d * TURNS)
            chosen.append((flag[dz, dc], before, first_early + d * NC + dc))
            before = before + flag[dz, dc]
        own_early.append(chosen)
    rows = []
    turns = lane_row.astype(f32)
    own_key, own_rank = column(key.astype(f32), me), column(rank, me)
    for d in range(2):
        turn = 1 if d == 0 else -1
        mine = (own_key < 64.0) if d == 0 else ((own_key >= 64.0) & (own_key < 1000.0))
        source = jnp.sum(jnp.where(mine & (own_rank == turns), blockf, 0.0), axis=0, keepdims=True)
        before = (me - turn * STRIDE + RING) % RING
        begin = column(starts[d, "early", 1], me)
        for here, seat_no, held_at in own_early[d]:
            at = begin + column(seat_no, me)
            source = jnp.where((column(here, me) > 0) & (turns == at), float(held_at), source)
        for kind, k in ORDER:
            if k > 1:
                begin, length = column(starts[d, kind, k], me), column(lengths[d, kind, k], me)
                old = column(starts[d, kind, k - 1], before)
                inside = (turns >= begin) & (turns < begin + length)
                source = jnp.where(inside, turns - begin + old + (n_blk + d * TURNS), source)
        rows.append(source)
    group = lane_row // (NX * NC)
    owner_cols = jnp.zeros((n_blk, RING), f32)
    spot_cols = jnp.zeros((n_blk, RING), f32)
    ownersf = owners.astype(f32)
    for g in range(NZ):
        dz = (g + 1) // 2 if g % 2 else (NZ - g // 2) % NZ
        origin = (me - dz * STRIDE + RING) % RING
        owner_cols = jnp.where(group == g, column(ownersf, origin), owner_cols)
        spot_cols = jnp.where(group == g, column(spot, origin), spot_cols)
    local = lane_row % (NX * NC)
    dest = (z * NX + (x + local // NC) % NX) * NC + (c + local % NC) % NC
    found = (owner_cols == dest.astype(f32)) & (spot_cols >= 0.0)
    place = jnp.sum(jnp.where(found, spot_cols, 0.0), axis=0, keepdims=True)
    for dz in EARLY_DZ:
        g = 2 * dz - 1 if dz <= half else 2 * (NZ - dz)
        origin = (me - dz * STRIDE + RING) % RING
        for dc in range(NC):
            lands = column(jnp.where(flag[dz, dc] > 0, early_spot[dz, dc], 0.0), origin)
            place = jnp.where(lane_row == g * SIDE + (NX // 2) * NC + dc, lands, place)
    rows.append(place)
    limits = jnp.clip(counts - block * BLOCK, 0, BLOCK).astype(f32)
    rows.append(jnp.sum(jnp.where(owners == tile, limits, 0.0), axis=0, keepdims=True))
    pick = jnp.zeros((1, RING), f32)
    for entry in second:
        pick = jnp.where(lane_row == entry, 1.0, pick)
    rows.append(pick)
    rows.append(jnp.broadcast_to(jnp.max(over, axis=1, keepdims=True), (1, RING)))
    own_owner = column(ownersf, me)
    rows.append(jnp.sum(jnp.where(own_owner == turns, blockf, 0.0), axis=0, keepdims=True))
    early_row = jnp.zeros((1, RING), f32)
    for k, idx in enumerate(early_idx):
        early_row = jnp.where(lane_row == k, column(idx, me), early_row)
    rows.append(early_row)
    return jnp.concatenate(rows, axis=0).astype(i32)


def plan_kernel(list_ref, owners_ref, counts_ref, out_ref):
    tile, grp = lax.axis_index("tile"), lax.axis_index("grp")
    second = [list_ref[1, k] for k in range(list_ref.shape[1])]
    out_ref[...] = relay_plan(
        owners_ref[...], counts_ref[...], second, tile, grp, lambda a, n: pltpu.roll(a, n % RING, 1)
    )


def f32dot(a, b):
    return jnp.dot(a, b, preferred_element_type=jnp.float32)


def f32dot_nt(a, b):
    return lax.dot_general(a, b, NT, preferred_element_type=jnp.float32)


class Parts:
    def __init__(self, table, hbm, out_ref, work):
        (self.obs, *self.sources) = hbm
        (self.recv, self.bgs, self.okw, self.ovw, self.qw, self.kw, self.vw, self.ow) = work[:8]
        (self.qbd, self.ovwt, self.vwt, self.acc, self.tot) = work[8:13]
        (self.load_sem, self.bsend_sem, self.brecv_sem) = work[13:]
        self.table, self.out_ref = table, out_ref
        self.tile, self.grp = lax.axis_index("tile"), lax.axis_index("grp")
        self.z, self.x, self.c = self.tile // SIDE, (self.tile // NC) % NX, self.tile % NC

    def at(self, dz, dx, dc):
        zz, xx, cc = (self.z + dz + NZ) % NZ, (self.x + dx + NX) % NX, (self.c + dc) % NC
        return (zz * NX + xx) * NC + cc

    def loads(self, obs_target):
        targets = (self.okw, self.ovw, self.bgs.at[0], self.qw, self.kw, self.vw, self.ow)
        pairs = [(self.obs, obs_target)] + list(zip(self.sources, targets))
        return [pltpu.make_async_copy(a, b, self.load_sem.at[k]) for k, (a, b) in enumerate(pairs)]

    def bg_copy(self, i):
        return pltpu.make_async_remote_copy(
            src_ref=self.bgs.at[0],
            dst_ref=self.bgs.at[i],
            send_sem=self.bsend_sem.at[i - 1],
            recv_sem=self.brecv_sem.at[i - 1],
            device_id=(self.tile, (self.grp + i) % NG),
            device_id_type=MESH,
        )

    def setup(self):
        self.ovwt[...] = self.ovw[...].T
        self.vwt[...] = self.vw[...].T
        qt = f32dot_nt(self.qw[...].T, self.bgs[0]).astype(jnp.bfloat16)
        self.qbd[...] = jnp.zeros_like(self.qbd)
        for b in range(2):
            for h in range(HEADS):
                half = h % 2
                rows, lanes = slice(half * HDIM, (half + 1) * HDIM), slice(half * BLOCK, (half + 1) * BLOCK)
                self.qbd[b, h // 2, rows, lanes] = qt[h * HDIM : (h + 1) * HDIM, b * BLOCK : (b + 1) * BLOCK]
        self.acc[...] = jnp.zeros_like(self.acc)
        self.tot[...] = jnp.zeros_like(self.tot)

    def weights(self, keys, p, pick):
        s = f32dot(keys[:, p * 2 * HDIM : (p + 1) * 2 * HDIM], self.qbd[pick, p])
        capped = jnp.tanh(s * (1.0 / (8.0 * SOFT_LIMIT)))
        return jnp.exp2(capped * (SOFT_LIMIT * LOG2E)).astype(jnp.bfloat16)

    def mix(self, vt, mask_rows, w, p):
        o = f32dot(jnp.concatenate([vt[p * 2 * HDIM : (p + 1) * 2 * HDIM], mask_rows], axis=0), w)
        return o[:HDIM, :BLOCK], o[HDIM : 2 * HDIM, BLOCK:], o[2 * HDIM : 2 * HDIM + 8]

    def add(self, b, p, terms):
        self.acc[b, 2 * p] += sum(t[0] for t in terms)
        self.acc[b, 2 * p + 1] += sum(t[1] for t in terms)
        self.tot[b, p] += sum(t[2] for t in terms)

    def latent_step(self, j, carry):
        rows = self.bgs[j]
        keys = f32dot(rows, self.kw[...]).astype(jnp.bfloat16)
        vt = f32dot_nt(self.vwt[...], rows).astype(jnp.bfloat16)
        ones = jnp.ones((16, 2 * BLOCK), jnp.bfloat16)
        ws = {(b, p): self.weights(keys, p, b) for p in range(PAIRS) for b in range(2)}
        for p in range(PAIRS):
            for b in range(2):
                self.add(b, p, [self.mix(vt, ones, ws[b, p], p)])
        return carry

    def slot_way(self, i):
        g, o = i // SIDE, i % SIDE
        dz = jnp.where(g % 2 == 1, (g + 1) // 2, (NZ - g // 2) % NZ)
        return dz, o // NC, o % NC

    def slot_math(self, first):
        picks, blocks, masks = [], [], []
        for k in range(BATCH):
            dz, dx, dc = self.slot_way(first + k)
            source = self.at(-dz, -dx, -dc)
            rows_ok = self.table[3, source * NG + self.grp]
            picks.append(self.table[4, source])
            row_id = lax.broadcasted_iota(jnp.int32, (BLOCK, CHANNELS), 0)
            block = self.recv[first + k]
            blocks.append(jnp.where(row_id < rows_ok, block, jnp.zeros_like(block)))
            lane_id = lax.broadcasted_iota(jnp.int32, (16, BLOCK), 1)
            masks.append(jnp.where(lane_id < rows_ok, 1.0, 0.0).astype(jnp.bfloat16))
        rows = jnp.concatenate(blocks, axis=0)
        keys = f32dot(rows, self.okw[...]).astype(jnp.bfloat16)
        vt = f32dot_nt(self.ovwt[...], rows).astype(jnp.bfloat16)
        part = [slice(k * BLOCK, (k + 1) * BLOCK) for k in range(BATCH)]
        ws = {(p, k): self.weights(keys[part[k]], p, picks[k]) for p in range(PAIRS) for k in range(BATCH)}
        for p in range(PAIRS):
            terms = [self.mix(vt[:, part[k]], masks[k], ws[p, k], p) for k in range(BATCH)]
            for b in range(2):
                self.add(b, p, [[jnp.where(picks[k] == b, v, 0.0) for v in terms[k]] for k in range(BATCH)])

    def result(self):
        for b in range(2):
            parts = []
            for h in range(HEADS):
                total = self.tot[b, h // 2, 0:1, (h % 2) * BLOCK : (h % 2 + 1) * BLOCK]
                parts.append(self.acc[b, h] / total)
            mixture = jnp.concatenate(parts, axis=0)
            scale = lax.rsqrt(jnp.mean(mixture * mixture, axis=0, keepdims=True) + EPSILON)
            normed = (mixture * scale).T.astype(jnp.bfloat16)
            rows = slice(b * BLOCK, (b + 1) * BLOCK)
            update = f32dot(normed, self.ow[...])
            self.out_ref[rows, :] = (self.bgs[0, rows, :].astype(jnp.float32) + update).astype(jnp.bfloat16)


def slot_copier(me, packed, send_sem, recv_sem):
    def slot_copy(i, dest):
        return pltpu.make_async_remote_copy(
            src_ref=packed.at[i],
            dst_ref=me.recv.at[i],
            send_sem=send_sem.at[i],
            recv_sem=recv_sem.at[i],
            device_id=(dest, me.grp),
            device_id_type=MESH,
        )

    return slot_copy


def direct_kernel(table, *refs):
    hbm, out_ref, (held, packed, send_sem, recv_sem), work = refs[:8], refs[8], refs[9:13], refs[13:]
    me = Parts(table, hbm, out_ref, work)
    loads = me.loads(held)
    for load in loads:
        load.start()
    barrier = pltpu.get_barrier_semaphore()

    def greet(i, carry):
        pl.semaphore_signal(barrier, inc=1, device_id=((me.tile + i) % SLOTS, me.grp), device_id_type=MESH)
        return carry

    lax.fori_loop(1, SLOTS, greet, 0)
    for i in range(1, NG):
        pl.semaphore_signal(barrier, inc=1, device_id=(me.tile, (me.grp + i) % NG), device_id_type=MESH)
    for load in loads:
        load.wait()
    pl.semaphore_wait(barrier, SLOTS - 1 + NG - 1)
    slot_copy = slot_copier(me, packed, send_sem, recv_sem)
    for i in range(1, NG):
        me.bg_copy(i).start()

    def send(i, carry):
        dest = me.at(*me.slot_way(i))
        block = held[table[6, dest]]

        @pl.when(i == 0)
        def _():
            me.recv[i] = block

        @pl.when(i > 0)
        def _():
            packed[i] = block
            slot_copy(i, dest).start()

        return carry

    lax.fori_loop(0, SLOTS, send, 0)
    me.setup()
    for i in range(1, NG):
        me.bg_copy(i).wait_recv()
    lax.fori_loop(0, NG, me.latent_step, 0)

    def step(n, carry):
        for k in range(BATCH):

            @pl.when(n * BATCH + k > 0)
            def _():
                slot_copy(n * BATCH + k, me.tile).wait_recv()

        me.slot_math(n * BATCH)
        return carry

    lax.fori_loop(0, SLOTS // BATCH, step, 0)
    me.result()

    def finish(i, carry):
        slot_copy(i, me.tile).wait_send()
        return carry

    lax.fori_loop(1, SLOTS, finish, 0)
    for i in range(1, NG):
        me.bg_copy(i).wait_send()


def reached(m, marks):
    return sum(jnp.where(m >= mark, 1, 0) for mark in marks)


LATENT_MARKS = (3, 5, 6, 7)
BATCH_MARKS = (8, 9, 14, 15, 16, 17, 19, 20, 21)
GROUP_MARKS = (0, 11, 11, 16, 16, 20, 20, 22)


def relay_kernel(table, *refs):
    hbm, out_ref = refs[:8], refs[8]
    (held, leaving, landing, packed, ahead, ahead_in) = refs[9:15]
    (send_sem, recv_sem, zsend_sem, zrecv_sem, asend_sem, arecv_sem), work = refs[15:21], refs[21:]
    me = Parts(table, hbm, out_ref, work)
    loads = me.loads(held.at[pl.ds(0, OBS_BLOCKS)])
    for load in loads:
        load.start()
    barrier = pltpu.get_barrier_semaphore()
    ring = (me.at(1, 0, 0), me.at(-1, 0, 0))
    peers = [(t, me.grp) for t in ring]
    peers += [(me.at(0, o // NC, o % NC), me.grp) for o in range(1, SIDE)]
    peers += [(me.tile, (me.grp + i) % NG) for i in range(1, NG)]
    for peer in peers:
        pl.semaphore_signal(barrier, inc=1, device_id=peer, device_id_type=MESH)
    loads[0].wait()
    pl.semaphore_wait(barrier, len(peers))
    slot_copy = slot_copier(me, packed, send_sem, recv_sem)

    def ring_copy(d, m):
        return pltpu.make_async_remote_copy(
            src_ref=leaving.at[d, m],
            dst_ref=landing.at[d, m],
            send_sem=zsend_sem.at[d, m],
            recv_sem=zrecv_sem.at[d, m],
            device_id=(ring[d], me.grp),
            device_id_type=MESH,
        )

    def early_copy(n):
        return pltpu.make_async_remote_copy(
            src_ref=ahead.at[n],
            dst_ref=ahead_in.at[n],
            send_sem=asend_sem.at[n],
            recv_sem=arecv_sem.at[n],
            device_id=(me.at(0, NX // 2, n % NC), me.grp),
            device_id_type=MESH,
        )

    def stays(i):
        return (i % SIDE == 0) | comes_early(i)

    def comes_early(i):
        return (i >= (2 * FAR - 1) * SIDE) & (i < (2 * FAR + 1) * SIDE) & ((i % SIDE) // NC == NX // 2)

    def side_send(i, carry):
        block = held[table[2, i]]
        o = i % SIDE

        @pl.when(o == 0)
        def _():
            me.recv[i] = block

        @pl.when(jnp.logical_not(stays(i)))
        def _():
            packed[i] = block
            slot_copy(i, me.at(0, o // NC, o % NC)).start()

        return carry

    def slot_step(n, carry):
        for k in range(BATCH):

            @pl.when(jnp.logical_not(stays(n * BATCH + k)))
            def _():
                slot_copy(n * BATCH + k, me.tile).wait_recv()

        me.slot_math(n * BATCH)
        return carry

    def step(m, carry):
        @pl.when(m >= BEHIND)
        def _():
            for d in range(2):
                ring_copy(d, m - BEHIND).wait_recv()
                for k in range(CHUNK):
                    held[OBS_BLOCKS + d * TURNS + (m - BEHIND) * CHUNK + k] = landing[d, m - BEHIND, k]

        @pl.when(m == EARLY_STEP)
        def _():
            for n in range(EARLY):
                early_copy(n).wait_recv()
                held[OBS_BLOCKS + 2 * TURNS + n] = ahead_in[n]

        @pl.when(m < CHUNKS)
        def _():
            for d in range(2):
                for k in range(CHUNK):
                    leaving[d, m, k] = held[table[d, m * CHUNK + k]]
                ring_copy(d, m).start()

        @pl.when(m == 0)
        def _():
            for n in range(EARLY):
                far, dc = n // NC, n % NC
                ahead[n] = held[table[7, far * NC + (me.c + dc) % NC]]
                early_copy(n).start()

        lax.fori_loop(reached(m - 1, GROUP_MARKS) * SIDE, reached(m, GROUP_MARKS) * SIDE, side_send, 0)

        @pl.when(m == 1)
        def _():
            for load in loads[1:]:
                load.wait()
            for i in range(1, NG):
                me.bg_copy(i).start()
            me.setup()

        @pl.when(m == LATENT_MARKS[1])
        def _():
            for i in range(1, NG):
                me.bg_copy(i).wait_recv()

        lax.fori_loop(reached(m - 1, LATENT_MARKS), reached(m, LATENT_MARKS), me.latent_step, 0)
        lax.fori_loop(reached(m - 1, BATCH_MARKS), reached(m, BATCH_MARKS), slot_step, 0)
        return carry

    lax.fori_loop(0, CHUNKS + BEHIND, step, 0)
    for g in (2 * FAR - 1, 2 * FAR):
        for dc in range(NC):
            i = g * SIDE + (NX // 2) * NC + dc
            me.recv[i] = held[table[2, i]]
    lax.fori_loop(len(BATCH_MARKS), SLOTS // BATCH, slot_step, 0)
    me.result()

    def finish(i, carry):
        @pl.when(jnp.logical_not(stays(i)))
        def _():
            slot_copy(i, me.tile).wait_send()

        return carry

    lax.fori_loop(0, SLOTS, finish, 0)

    def ring_finish(m, carry):
        for d in range(2):
            ring_copy(d, m).wait_send()
        return carry

    lax.fori_loop(0, CHUNKS, ring_finish, 0)
    for n in range(EARLY):
        early_copy(n).wait_send()
    for i in range(1, NG):
        me.bg_copy(i).wait_send()


def exchange_call(kernel, collective_id, own_scratch, name):
    bf16, f32 = jnp.bfloat16, jnp.float32
    smem = pl.BlockSpec(memory_space=pltpu.SMEM)
    vmem = pl.BlockSpec(memory_space=pltpu.VMEM)
    hbm = pl.BlockSpec(memory_space=pl.ANY)
    shared = [
        pltpu.VMEM((SLOTS, BLOCK, CHANNELS), bf16),
        pltpu.VMEM((NG, 2 * BLOCK, WIDTH), bf16),
        pltpu.VMEM((CHANNELS, WIDTH), bf16),
        pltpu.VMEM((CHANNELS, WIDTH), bf16),
        pltpu.VMEM((WIDTH, WIDTH), bf16),
        pltpu.VMEM((WIDTH, WIDTH), bf16),
        pltpu.VMEM((WIDTH, WIDTH), bf16),
        pltpu.VMEM((WIDTH, WIDTH), bf16),
        pltpu.VMEM((2, PAIRS, 2 * HDIM, 2 * BLOCK), bf16),
        pltpu.VMEM((WIDTH, CHANNELS), bf16),
        pltpu.VMEM((WIDTH, WIDTH), bf16),
        pltpu.VMEM((2, HEADS, HDIM, BLOCK), f32),
        pltpu.VMEM((2, PAIRS, 8, 2 * BLOCK), f32),
        pltpu.SemaphoreType.DMA((8,)),
        pltpu.SemaphoreType.DMA((NG - 1,)),
        pltpu.SemaphoreType.DMA((NG - 1,)),
    ]
    return pl.pallas_call(
        kernel,
        out_shape=jax.ShapeDtypeStruct((2 * BLOCK, WIDTH), bf16),
        in_specs=[smem] + [hbm] * 8,
        out_specs=vmem,
        scratch_shapes=own_scratch + shared,
        compiler_params=pltpu.CompilerParams(
            collective_id=collective_id, has_side_effects=True, vmem_limit_bytes=48 * 1024 * 1024
        ),
        cost_estimate=pl.CostEstimate(flops=12_000_000_000, bytes_accessed=8_000_000, transcendentals=21_000_000),
        name=name,
    )


def slots_of(count):
    return pltpu.VMEM((count, BLOCK, CHANNELS), jnp.bfloat16)


def local(
    observations,
    obs_key_weight,
    obs_value_weight,
    background,
    query_weight,
    key_weight,
    value_weight,
    out_weight,
    owners,
    attend_list,
    obs_count,
):
    vmem = pl.BlockSpec(memory_space=pltpu.VMEM)
    table = pl.pallas_call(
        plan_kernel,
        out_shape=jax.ShapeDtypeStruct((8, RING), jnp.int32),
        in_specs=[pl.BlockSpec(memory_space=pltpu.SMEM), vmem, vmem],
        out_specs=vmem,
        name="plan",
    )(attend_list, owners.T, obs_count[None, :])
    dma = pltpu.SemaphoreType.DMA
    relay = exchange_call(
        relay_kernel,
        0,
        [
            slots_of(OBS_BLOCKS + 2 * TURNS + EARLY),
            pltpu.VMEM((2, CHUNKS, CHUNK, BLOCK, CHANNELS), jnp.bfloat16),
            pltpu.VMEM((2, CHUNKS, CHUNK, BLOCK, CHANNELS), jnp.bfloat16),
            slots_of(SLOTS),
            slots_of(EARLY),
            slots_of(EARLY),
            dma((SLOTS,)),
            dma((SLOTS,)),
            dma((2, CHUNKS)),
            dma((2, CHUNKS)),
            dma((EARLY,)),
            dma((EARLY,)),
        ],
        "relay",
    )
    direct = exchange_call(
        direct_kernel, 1, [slots_of(OBS_BLOCKS), slots_of(SLOTS), dma((SLOTS,)), dma((SLOTS,))], "direct"
    )
    operands = (
        table,
        observations.reshape(OBS_BLOCKS, BLOCK, CHANNELS),
        obs_key_weight,
        obs_value_weight,
        background,
        query_weight,
        key_weight,
        value_weight,
        out_weight,
    )
    return lax.cond(table[5, 0] <= 0, lambda *a: relay(*a), lambda *a: direct(*a), *operands)


def solution(mesh):
    rows = P(("tile", "grp"), None)
    in_specs = (rows, P(), P(), rows, P(), P(), P(), P(), P(), rows, P())
    return jax.shard_map(local, mesh=mesh, in_specs=in_specs, out_specs=rows, check_vma=False)
```
